32 devices in a mesh: grp: 2 (over y), section: 2 (over core), seq: 4 (over z), fsdp: 2 (over x).
Axes of the slice: x: 2, y: 2, z: 4, core: 2. Of those that a mesh axis runs over, the one named last changes fastest.
Arguments:
- head_inputs: bfloat16 [2, 4, 256, 7680], P('section', ('grp', 'fsdp'), 'seq'), parts along dimension 1, may hold values from -8 to 8
- hidden: bfloat16 [2, 4, 256, 2560], P('section', ('grp', 'fsdp'), 'seq'), parts along dimension 1, may hold values from -3 to 3
- out_weight: bfloat16 [2, 2560, 2560], P('section', 'fsdp'), may hold values from -0.125 to 0.125
- time_weight: bfloat16 [2, 256, 7680], P('section', None, ('seq', 'fsdp')), may hold values from -0.375 to 0.375
- head_weight: bfloat16 [2, 2560, 64], P('section', ('seq', 'fsdp')), may hold values from -0.125 to 0.125
- latent: float32 [2, 4, 128, 128], P('section', ('grp', 'fsdp'), 'seq'), parts along dimension 1, may hold values from -6 to 6
- timesteps: int32 [2, 4, 2], P('section', ('grp', 'fsdp')), parts along dimension 1, may hold values from 41 to 999, as said below
Outputs:
- velocity: float32 [2, 4, 128, 128], P('section', ('grp', 'fsdp'), 'seq'), parts along dimension 1
- carried: float32 [2, 4, 128, 128], P('section', ('grp', 'fsdp'), 'seq'), parts along dimension 1
The draws below stay inside these ranges and needn't reach their ends.
There are 2 independent parts, one for each index of `grp`. The reference program is written for one: setup_inputs(seed, part) draws one part's arguments, and reference() takes and returns one part's arrays. A program takes and returns all parts, laid end to end along the dimension named above; an argument that names none is the same for every part. Nothing has to cross between parts.
Inputs may be any that keep to these rules, and one draw needn't show every extreme that they name: timesteps[0] lie in 875 to 999 and timesteps[1] in 100 to 874 for the current entry; the next entry is the current one minus 10 to 59.
All inputs are finite; a program needn't handle non-finite values.
Results may differ from the reference program's by a relative error of at most 0.0049.
Values may be sent and summed in bfloat16 or wider, within the bound.
A program may use at most 128 MiB of HBM per device.

```python
import math
import jax
import jax.numpy as jnp
from jax import lax

DIM = 2560
HEADS = 32
HEAD = 80
PATCH = 64
FREQ = 256
BATCH = 2
SEQLEN = 256


def draw_head_inputs(key, part):
    key_base = jax.random.fold_in(key, 11)
    shape = (2, BATCH, SEQLEN, HEADS, 3, HEAD)
    spreads = jnp.array([1.5, 1.5, 1.0], jnp.float32)[:, None]
    base = jnp.clip(jax.random.normal(key_base, shape, jnp.float32) * spreads, -8.0, 8.0)
    return base.reshape(2, BATCH, SEQLEN, HEADS * 3 * HEAD).astype(jnp.bfloat16)


def draw_timesteps(key, part):
    key_high = jax.random.fold_in(key, 21)
    key_low = jax.random.fold_in(key, 22)
    key_gap = jax.random.fold_in(key, 23)
    high_steps = jax.random.randint(key_high, (BATCH,), 875, 1000)
    low_steps = jax.random.randint(key_low, (BATCH,), 100, 875)
    current = jnp.stack([high_steps, low_steps]).astype(jnp.int32)
    gaps = jax.random.randint(key_gap, (2, BATCH), 10, 60).astype(jnp.int32)
    return jnp.stack([current, current - gaps], axis=-1).astype(jnp.int32)


def block_scale(rng, extent, split, smallest, top_value):
    level = 1.0
    for dim, shards_of in split:
        draws = jax.random.uniform(jax.random.fold_in(jax.random.fold_in(rng, 6), dim), (shards_of,), jnp.float32, smallest / len(split), top_value / len(split))
        level = level * jnp.repeat(jnp.exp(draws), extent[dim] // shards_of).reshape((-1,) + (1,) * (len(extent) - 1 - dim))
    return level


def bell_draw(rng, extent, deviation, most, cuts=(), held_as=jnp.bfloat16):
    loudness = block_scale(rng, extent, cuts, -0.22, 0.18) if cuts else 1.0
    result = jax.random.normal(rng, extent, jnp.float32) * deviation * loudness
    return jnp.minimum(jnp.maximum(result, -most), most).astype(held_as)


def setup_inputs(seed: int = 0, part: int = 0) -> dict:
    splits = jax.random.split(jax.random.key(seed), 8)
    part_keys = jax.random.split(jax.random.fold_in(splits[7], part), 8)
    return {
        "head_inputs": draw_head_inputs(jax.random.fold_in(jax.random.fold_in(splits[7], part), 71), part),
        "hidden": bell_draw(part_keys[1], (2, BATCH, SEQLEN, DIM), 0.5, 3.0, ((0, 2), (1, 2), (2, 4))),
        "out_weight": bell_draw(splits[2], (2, HEADS * HEAD, DIM), (HEADS * HEAD) ** -0.5, 0.125, ((0, 2), (1, 2))),
        "time_weight": bell_draw(splits[3], (2, FREQ, 3 * DIM), FREQ ** -0.5, 0.375, ((0, 2), (2, 8))),
        "head_weight": bell_draw(splits[4], (2, DIM, PATCH), DIM ** -0.5, 0.125, ((0, 2), (1, 8))),
        "latent": bell_draw(part_keys[5], (2, BATCH, SEQLEN // 2, 2 * PATCH), 1.0, 6.0, ((0, 2), (1, 2), (2, 4)), jnp.float32),
        "timesteps": draw_timesteps(jax.random.fold_in(jax.random.fold_in(splits[7], part), 71), part),
    }


def time_embed(steps_now):
    half = FREQ // 2
    freqs = jnp.exp(-math.log(10000.0) * jnp.arange(half, dtype=jnp.float32) / half)
    angle = steps_now.astype(jnp.float32)[..., None] * freqs
    return jnp.concatenate([jnp.cos(angle), jnp.sin(angle)], axis=-1)

def sigma_of(steps_now):
    unit_time = steps_now.astype(jnp.float32) / 1000.0
    return 5.0 * unit_time / (1.0 + 4.0 * unit_time)

def head_attention(group):
    query_rows = group[0]
    key_rows = group[1]
    value_rows = group[2]
    scores = jnp.dot(query_rows, key_rows.T, preferred_element_type=jnp.float32) * HEAD ** (-0.5)
    row_max = lax.optimization_barrier(jnp.max(scores, axis=-1, keepdims=True))
    exp_scores = jnp.exp(scores - row_max)
    row_sum = lax.optimization_barrier(jnp.sum(exp_scores, axis=-1, keepdims=True))
    weights = (exp_scores / row_sum).astype(jnp.bfloat16)
    return jnp.dot(weights, value_rows, preferred_element_type=jnp.float32).astype(jnp.bfloat16)

def reference(head_inputs, hidden, out_weight, time_weight, head_weight, latent, timesteps):

    def per_section(section_in):
        section_heads, section_hidden, section_out, section_time, section_head, section_latent, section_steps = section_in

        def per_sample(sample_in):
            item_heads, item_hidden, item_latent, item_steps = sample_in
            grouped = item_heads.reshape(SEQLEN, HEADS, 3, HEAD).transpose(1, 2, 0, 3)
            per_head = lax.map(head_attention, grouped)
            attended = per_head.transpose(1, 0, 2).reshape(SEQLEN, HEADS * HEAD)
            embedding = time_embed(item_steps[0]).astype(jnp.bfloat16)
            modulation = jnp.dot(embedding[None, :], section_time, preferred_element_type=jnp.float32)[0]
            gate_term = modulation[:DIM]
            shift_term = modulation[DIM:2 * DIM]
            scale_term = modulation[2 * DIM:]
            projected = jnp.dot(attended, section_out, preferred_element_type=jnp.float32)
            updated = item_hidden.astype(jnp.float32) + gate_term * projected
            average = lax.optimization_barrier(jnp.mean(updated, axis=-1, keepdims=True))
            centred = updated - average
            variance = lax.optimization_barrier(jnp.mean(centred * centred, axis=-1, keepdims=True))
            normed = (centred * lax.rsqrt(variance + 1e-06) * (1.0 + scale_term) + shift_term).astype(jnp.bfloat16)
            velocity = jnp.dot(normed, section_head, preferred_element_type=jnp.float32)
            velocity = velocity.reshape(SEQLEN // 2, 2 * PATCH)
            step_size = sigma_of(item_steps[1]) - sigma_of(item_steps[0])
            stepped = item_latent + step_size * velocity
            return (velocity, stepped)
        return lax.map(per_sample, (section_heads, section_hidden, section_latent, section_steps))
    velocity, stepped = lax.map(per_section, (head_inputs, hidden, out_weight, time_weight, head_weight, latent, timesteps))
    carried = jnp.stack([stepped[1], stepped[0]])
    return (velocity, carried)
```

```python
import functools
import math

import jax
import jax.numpy as jnp
import numpy as np
from jax import lax
from jax.experimental import pallas as pl
from jax.experimental.pallas import tpu as pltpu
from jax.sharding import PartitionSpec as P

DIM = 2560
HEADS = 32
HEAD = 80
PATCH = 64
FREQ = 256


def partner(block, axis, apart):
    count = lax.axis_size(axis)
    route = []
    for low in range(count):
        high = low | 1 << apart
        if high != low and high < count:
            route += [(low, high), (high, low)]
    return lax.ppermute(block, axis, route)


def time_embed(steps_now):
    half = FREQ // 2
    freqs = jnp.exp(-math.log(10000.0) * jnp.arange(half, dtype=jnp.float32) / half)
    angle = steps_now.astype(jnp.float32)[..., None] * freqs
    return jnp.concatenate([jnp.cos(angle), jnp.sin(angle)], axis=-1)


def sigma_of(steps_now):
    unit_time = steps_now.astype(jnp.float32) / 1000.0
    return 5.0 * unit_time / (1.0 + 4.0 * unit_time)


def attend(exchanged):
    items = exchanged.shape[0]
    length = exchanged.shape[1]
    local_heads = exchanged.shape[2]
    query_all = exchanged[..., :HEAD]
    key_rows = exchanged[..., HEAD : 2 * HEAD]
    value_rows = exchanged[..., 2 * HEAD :]
    block_rows = min(512, length)
    block_count = length // block_rows

    def one_block(block_index):
        query_block = lax.dynamic_slice_in_dim(query_all, block_index * block_rows, block_rows, 1)
        scores = jnp.einsum(
            "nqhe,nkhe->nhqk", query_block, key_rows, preferred_element_type=jnp.float32
        ) * HEAD ** (-0.5)
        row_max = jnp.max(scores, axis=-1, keepdims=True)
        exp_scores = jnp.exp(scores - row_max)
        row_sum = jnp.sum(exp_scores, axis=-1, keepdims=True)
        weights = (exp_scores / row_sum).astype(jnp.bfloat16)
        return jnp.einsum(
            "nhqk,nkhe->nqhe", weights, value_rows, preferred_element_type=jnp.float32
        ).astype(jnp.bfloat16)

    blocks = lax.map(one_block, jnp.arange(block_count, dtype=jnp.int32))
    return blocks.transpose(1, 0, 2, 3, 4).reshape(items, length, local_heads * HEAD)


def body(head_inputs, hidden, out_weight, time_weight, head_weight, latent, timesteps):
    samples = head_inputs.shape[1]
    row_count = head_inputs.shape[2]
    flat_count = samples * row_count
    local = head_inputs.reshape(samples, row_count, HEADS, 3 * HEAD)
    attended = lax.all_to_all(
        attend(lax.all_to_all(local, "seq", split_axis=2, concat_axis=1, tiled=True)),
        "seq",
        split_axis=1,
        concat_axis=2,
        tiled=True,
    )
    flattened = attended.reshape(flat_count, HEADS * HEAD)
    time_full, head_full = (
        lax.all_gather(time_weight, ("seq", "fsdp"), axis=2, tiled=True),
        lax.all_gather(head_weight, ("seq", "fsdp"), axis=1, tiled=True),
    )
    embedding = time_embed(timesteps[0, :, 0]).astype(jnp.bfloat16)
    modulation = jnp.dot(embedding, time_full[0], preferred_element_type=jnp.float32)
    gate_term = modulation[:, None, :DIM]
    shift_term = modulation[:, None, DIM : 2 * DIM]
    scale_term = modulation[:, None, 2 * DIM :]
    own_columns = lax.all_to_all(flattened, "fsdp", split_axis=1, concat_axis=0, tiled=True)
    projected = lax.psum_scatter(
        jnp.dot(own_columns, out_weight[0], preferred_element_type=jnp.float32).astype(
            jnp.bfloat16
        ),
        "fsdp",
        scatter_dimension=0,
        tiled=True,
    ).astype(jnp.float32)
    updated = hidden.reshape(samples, row_count, DIM).astype(
        jnp.float32
    ) + gate_term * projected.reshape(samples, row_count, DIM)
    average = jnp.mean(updated, axis=-1, keepdims=True)
    centred = updated - average
    variance = jnp.mean(centred * centred, axis=-1, keepdims=True)
    normed = (centred * lax.rsqrt(variance + 1e-06) * (1.0 + scale_term) + shift_term).astype(
        jnp.bfloat16
    )
    velocity = jnp.dot(
        normed.reshape(flat_count, DIM), head_full[0], preferred_element_type=jnp.float32
    )
    velocity = velocity.reshape(1, samples, row_count // 2, 2 * PATCH)
    step_size = sigma_of(timesteps[0, :, 1]) - sigma_of(timesteps[0, :, 0])
    stepped = latent + step_size[None, :, None, None] * velocity
    carried = partner(stepped, "section", 0)
    return (velocity, carried)


MESH = pl.DeviceIdType.MESH
BF16 = jnp.bfloat16
F32 = jnp.float32


def up(value, step):
    return -(-value // step) * step


class Plan:
    def __init__(self, seq, fsdp, rows):
        self.seq, self.fsdp, self.rows = seq, fsdp, rows
        self.heads = HEADS // seq
        self.group_in = self.heads * 3 * HEAD
        self.group_out = self.heads * HEAD
        per = max(1, self.heads // 4)
        self.chunks = []
        lo_in = lo_out = 0
        for first in range(0, self.heads, per):
            last = min(first + per, self.heads)
            hi_in = min(up(last * 3 * HEAD, 128), self.group_in)
            hi_out = last * HEAD // 128 * 128 if last < self.heads else self.group_out
            self.chunks.append((first, last, (lo_in, hi_in), (lo_out, hi_out)))
            lo_in, lo_out = hi_in, hi_out
        self.block = 512
        self.blocks = DIM // self.block


def fused(
    plan, qkv, hid, ow, tw, hw, lat, ts, freqs, vel_out, car_out,
    qkv_v, ow_v, tw_v, hw_v, hid_v, lat_v, emb, mod_loc, mod_all, att, gath, own, part, got, packed, head_v,
    upd, vel_v, step_v, step_in,
    loc_sem, own_sem, qs, qr, es, er, ms, mr, hxs, hxr, hzs, hzr, as_, ar, ps, pr, cs, cr,
):
    seq, fsdp, rows = plan.seq, plan.fsdp, plan.rows
    z, f, s = lax.axis_index("seq"), lax.axis_index("fsdp"), lax.axis_index("section")
    other = 1 - f
    slot = z * fsdp + f
    per_half = seq // fsdp
    n_chunks = len(plan.chunks)

    def remote(src, dst, send, recv, to):
        return pltpu.make_async_remote_copy(
            src_ref=src, dst_ref=dst, send_sem=send, recv_sem=recv, device_id=to, device_id_type=MESH
        )

    barrier = pltpu.get_barrier_semaphore()
    for dz in range(seq):
        for df in range(fsdp):
            if dz or df:
                to = {"seq": z ^ dz, "fsdp": f ^ df}
                pl.semaphore_signal(barrier, inc=1, device_id=to, device_id_type=MESH)
    pl.semaphore_signal(barrier, inc=1, device_id={"section": 1 - s}, device_id_type=MESH)

    loads = [
        pltpu.make_async_copy(hw.at[0], hw_v, loc_sem.at[0]),
        pltpu.make_async_copy(tw.at[0], tw_v, loc_sem.at[1]),
        pltpu.make_async_copy(ow.at[0], ow_v, loc_sem.at[2]),
        pltpu.make_async_copy(hid.at[0, 0], hid_v, loc_sem.at[3]),
        pltpu.make_async_copy(lat.at[0, 0], lat_v, loc_sem.at[4]),
    ]

    def group_of(position):
        return lax.rem(position, fsdp) * per_half + position // fsdp

    def columns(position, span):
        first = group_of(position) * plan.group_in + span[0]
        return pl.ds(pl.multiple_of(first, 128), span[1] - span[0])

    def my_rows(position):
        return pl.ds(pl.multiple_of(position * rows, rows), rows)

    own_loads = []
    for c, (_, _, span, _) in enumerate(plan.chunks):
        own_loads.append(
            pltpu.make_async_copy(
                qkv.at[0, 0, :, columns(z, span)],
                qkv_v.at[my_rows(z), span[0] : span[1]],
                own_sem.at[c],
            )
        )
        own_loads[-1].start()
    for load in loads:
        load.start()

    t_now = ts[0, 0, 0].astype(F32)
    angle = t_now * jnp.broadcast_to(freqs[...], (8, FREQ // 2))
    emb[f, :, : FREQ // 2] = jnp.cos(angle)
    emb[f, :, FREQ // 2 :] = jnp.sin(angle)

    pl.semaphore_wait(barrier, seq * fsdp)

    order = sorted(range(1, seq), reverse=True)
    sends = []
    emb_copy = remote(emb.at[f], emb.at[f], es, er, {"fsdp": other})
    emb_copy.start()
    in_copies = []
    for c, (_, _, span, _) in enumerate(plan.chunks):
        row = []
        for d in order:
            peer = z ^ d
            row.append(
                remote(
                    qkv.at[0, 0, :, columns(peer, span)],
                    qkv_v.at[my_rows(z), span[0] : span[1]],
                    qs.at[c, d],
                    qr.at[c, d],
                    {"seq": peer},
                )
            )
            row[-1].start()
        in_copies.append(row)

    loads[0].wait()
    half_rows = hw_v.shape[0] // 2
    packed[slot] = jnp.concatenate([hw_v[:half_rows], hw_v[half_rows:]], axis=1)
    head_copy = remote(packed.at[slot], packed.at[slot], hxs, hxr, {"fsdp": other})
    head_copy.start()

    emb_copy.wait()
    loads[1].wait()
    both = emb[...].reshape(fsdp * 8, FREQ).astype(BF16)
    mod = jnp.dot(both, tw_v[...], preferred_element_type=F32)
    for b in range(fsdp):
        mod_loc[b] = mod[b * 8 : b * 8 + 1]
    mod_all[slot] = mod_loc[f]
    mod_copies = []
    for dz in range(seq):
        for df in range(fsdp):
            if dz or df:
                mod_copies.append(
                    remote(
                        mod_loc.at[f ^ df],
                        mod_all.at[slot],
                        ms.at[dz, df],
                        mr.at[dz, df],
                        {"seq": z ^ dz, "fsdp": f ^ df},
                    )
                )
                mod_copies[-1].start()

    half = lax.rem(z, fsdp)
    part_of_half = z // fsdp
    for c, (first, last, _, span) in enumerate(plan.chunks):
        own_loads[c].wait()
        for copy in in_copies[c]:
            copy.wait_recv()
        for h in range(first, last):
            base = h * 3 * HEAD
            query = qkv_v[:, base : base + HEAD]
            key = qkv_v[:, base + HEAD : base + 2 * HEAD]
            value = qkv_v[:, base + 2 * HEAD : base + 3 * HEAD]
            scores = lax.dot_general(
                query, key, (((1,), (1,)), ((), ())), preferred_element_type=F32
            ) * HEAD ** (-0.5)
            exps = jnp.exp(scores - jnp.max(scores, axis=-1, keepdims=True))
            weights = (exps * (1.0 / jnp.sum(exps, axis=-1, keepdims=True))).astype(BF16)
            att[:, h * HEAD : (h + 1) * HEAD] = jnp.dot(
                weights, value, preferred_element_type=F32
            ).astype(BF16)
        lo, hi = span
        for d in [*order, 0]:
            peer = z ^ d
            source = att.at[my_rows(peer), lo:hi]
            target = gath.at[f, part_of_half, :, lo:hi]
            if d:
                remote(
                    source, target, as_.at[c, d], ar.at[c, f, part_of_half], {"seq": peer, "fsdp": half}
                ).start()
            else:

                @pl.when(half == f)
                def _():
                    pltpu.make_async_copy(source, target, ar.at[c, f, part_of_half]).start()

                @pl.when(half != f)
                def _():
                    remote(
                        source, target, as_.at[c, d], ar.at[c, f, part_of_half], {"fsdp": half}
                    ).start()

    head_copy.wait()
    head_copies = []
    for d in order:
        for b, index in enumerate((slot, z * fsdp + other)):
            head_copies.append(
                remote(packed.at[index], packed.at[index], hzs.at[b, d], hzr.at[b, d], {"seq": z ^ d})
            )
            head_copies[-1].start()

    loads[2].wait()
    for c, (_, _, _, (lo, hi)) in enumerate(plan.chunks):
        for b in range(fsdp):
            for i in range(per_half):
                block = gath.at[b, i, :, lo:hi]
                pltpu.make_async_copy(block, block, ar.at[c, b, i]).wait()
    part_copies = []
    for k in range(plan.blocks):
        cols = slice(k * plan.block, (k + 1) * plan.block)
        total = jnp.zeros((fsdp * rows, plan.block), F32)
        for i in range(per_half):
            total += jnp.dot(
                gath[:, i].reshape(fsdp * rows, plan.group_out),
                ow_v[i * plan.group_out : (i + 1) * plan.group_out, cols],
                preferred_element_type=F32,
            )
        for b in range(fsdp):
            own[b, :, cols] = total[b * rows : (b + 1) * rows]
            part[b, :, cols] = total[b * rows : (b + 1) * rows].astype(BF16)
        part_copies.append(
            remote(part.at[other, :, cols], got.at[:, cols], ps.at[k], pr.at[k], {"fsdp": other})
        )
        part_copies[-1].start()

    for copy in head_copies:
        copy.wait_recv()
    for j in range(seq * fsdp):
        block = packed[j]
        swapped = jnp.concatenate([block[:, PATCH:], block[:, :PATCH]], axis=1)
        left = lax.broadcasted_iota(jnp.int32, block.shape, 1) < PATCH
        head_v[2 * half_rows * j : 2 * half_rows * j + half_rows] = jnp.where(left, block, swapped)
        head_v[2 * half_rows * j + half_rows : 2 * half_rows * (j + 1)] = jnp.where(
            left, swapped, block
        )
    for copy in mod_copies:
        copy.wait_recv()
    modulation = jnp.concatenate([mod_all[j] for j in range(seq * fsdp)], axis=1)
    gate = modulation[:, :DIM]
    shift = modulation[:, DIM : 2 * DIM]
    scale = modulation[:, 2 * DIM :]
    loads[3].wait()
    loads[4].wait()

    sums = jnp.zeros((rows, 1), F32)
    for k in range(plan.blocks):
        cols = slice(k * plan.block, (k + 1) * plan.block)
        part_copies[k].wait_recv()
        projected = own[f, :, cols] + got[:, cols].astype(F32)
        now = hid_v[:, cols].astype(F32) + gate[:, cols] * projected
        upd[:, cols] = now
        sums += jnp.sum(now, axis=-1, keepdims=True)
    centred = upd[...] - sums * (1.0 / DIM)
    variance = jnp.mean(centred * centred, axis=-1, keepdims=True)
    normed = (centred * lax.rsqrt(variance + 1e-06) * (1.0 + scale) + shift).astype(BF16)
    vel_v[...] = jnp.dot(normed, head_v[...], preferred_element_type=F32)
    even = vel_v[pl.ds(0, rows // 2, 2), :]
    odd = vel_v[pl.ds(1, rows // 2, 2), :]
    left = lax.broadcasted_iota(jnp.int32, even.shape, 1) < PATCH
    velocity = jnp.where(left, even, odd)
    vel_out[0, 0] = velocity

    unit = jnp.full((1, 2 * PATCH), ts[0, 0, 0].astype(F32), F32) / 1000.0
    unit_next = jnp.full((1, 2 * PATCH), ts[0, 0, 1].astype(F32), F32) / 1000.0
    step = 5.0 * unit_next / (1.0 + 4.0 * unit_next) - 5.0 * unit / (1.0 + 4.0 * unit)
    step_v[...] = lat_v[...] + step * velocity
    swap = remote(step_v, step_in, cs, cr, {"section": 1 - s})
    swap.start()

    for row in in_copies:
        for copy in row:
            copy.wait_send()
    for copy in mod_copies + head_copies + part_copies:
        copy.wait_send()
    for c, (_, _, _, (lo, hi)) in enumerate(plan.chunks):
        for d in order:
            block = att.at[0:rows, lo:hi]
            pltpu.make_async_copy(block, block, as_.at[c, d]).wait()

        @pl.when(half != f)
        def _():
            block = att.at[0:rows, lo:hi]
            pltpu.make_async_copy(block, block, as_.at[c, 0]).wait()

    swap.wait()
    car_out[0, 0] = step_in[...]


def fused_body(plan, head_inputs, hidden, out_weight, time_weight, head_weight, latent, timesteps):
    seq, fsdp, rows = plan.seq, plan.fsdp, plan.rows
    chunks = len(plan.chunks)
    per_half = seq // fsdp
    half = FREQ // 2
    freqs = np.exp(-math.log(10000.0) * np.arange(half) / half).astype(np.float32)[None]
    dma = pltpu.SemaphoreType.DMA
    vmem = pltpu.VMEM
    whole = pl.BlockSpec(memory_space=pltpu.VMEM)
    anywhere = pl.BlockSpec(memory_space=pl.ANY)
    parts = seq * fsdp
    return pl.pallas_call(
        functools.partial(fused, plan),
        out_shape=(
            jax.ShapeDtypeStruct(latent.shape, F32),
            jax.ShapeDtypeStruct(latent.shape, F32),
        ),
        in_specs=[anywhere] * 6 + [pl.BlockSpec(memory_space=pltpu.SMEM), whole],
        out_specs=(whole, whole),
        scratch_shapes=[
            vmem((seq * rows, plan.group_in), BF16),
            vmem(out_weight.shape[1:], BF16),
            vmem(time_weight.shape[1:], BF16),
            vmem(head_weight.shape[1:], BF16),
            vmem((rows, DIM), BF16),
            vmem(latent.shape[2:], F32),
            vmem((fsdp, 8, FREQ), F32),
            vmem((fsdp, 1, time_weight.shape[2]), F32),
            vmem((parts, 1, time_weight.shape[2]), F32),
            vmem((seq * rows, plan.group_out), BF16),
            vmem((fsdp, per_half, rows, plan.group_out), BF16),
            vmem((fsdp, rows, DIM), F32),
            vmem((fsdp, rows, DIM), BF16),
            vmem((rows, DIM), BF16),
            vmem((parts, head_weight.shape[1] // 2, 2 * PATCH), BF16),
            vmem((DIM, 2 * PATCH), BF16),
            vmem((rows, DIM), F32),
            vmem((rows, 2 * PATCH), F32),
            vmem(latent.shape[2:], F32),
            vmem(latent.shape[2:], F32),
            dma((5,)),
            dma((chunks,)),
            dma((chunks, seq)),
            dma((chunks, seq)),
            dma,
            dma,
            dma((seq, fsdp)),
            dma((seq, fsdp)),
            dma,
            dma,
            dma((fsdp, seq)),
            dma((fsdp, seq)),
            dma((chunks, seq)),
            dma((chunks, fsdp, per_half)),
            dma((plan.blocks,)),
            dma((plan.blocks,)),
            dma,
            dma,
        ],
        compiler_params=pltpu.CompilerParams(
            collective_id=0, has_side_effects=True, vmem_limit_bytes=40 * 2**20
        ),
        name="fused_step",
    )(head_inputs, hidden, out_weight, time_weight, head_weight, latent, timesteps, freqs)


def pick(mesh):
    seq, fsdp, sections = mesh.shape["seq"], mesh.shape["fsdp"], mesh.shape["section"]

    def run(*blocks):
        samples, rows = blocks[0].shape[1:3]
        fits = (
            samples == 1
            and fsdp == 2
            and sections == 2
            and seq & (seq - 1) == 0
            and seq % fsdp == 0
            and HEADS % seq == 0
            and (HEADS // seq * HEAD) % 128 == 0
            and rows % 16 == 0
            and seq * rows <= 512
            and (blocks[4].shape[1] // 2) % 16 == 0
        )
        if fits:
            return fused_body(Plan(seq, fsdp, rows), *blocks)
        return body(*blocks)

    return run


def solution(mesh):
    return jax.shard_map(
        pick(mesh),
        mesh=mesh,
        in_specs=(
            P("section", ("grp", "fsdp"), "seq", None),
            P("section", ("grp", "fsdp"), "seq", None),
            P("section", "fsdp", None),
            P("section", None, ("seq", "fsdp")),
            P("section", ("seq", "fsdp"), None),
            P("section", ("grp", "fsdp"), "seq", None),
            P("section", ("grp", "fsdp"), None),
        ),
        out_specs=(
            P("section", ("grp", "fsdp"), "seq", None),
            P("section", ("grp", "fsdp"), "seq", None),
        ),
        check_vma=False,
    )
```

```python
import functools
import math

import jax
import jax.numpy as jnp
import numpy as np
from jax import lax
from jax.experimental import pallas as pl
from jax.experimental.pallas import tpu as pltpu
from jax.sharding import PartitionSpec as P

DIM = 2560
HEADS = 32
HEAD = 80
PATCH = 64
FREQ = 256


def partner(block, axis, apart):
    count = lax.axis_size(axis)
    route = []
    for low in range(count):
        high = low | 1 << apart
        if high != low and high < count:
            route += [(low, high), (high, low)]
    return lax.ppermute(block, axis, route)


def time_embed(steps_now):
    half = FREQ // 2
    freqs = jnp.exp(-math.log(10000.0) * jnp.arange(half, dtype=jnp.float32) / half)
    angle = steps_now.astype(jnp.float32)[..., None] * freqs
    return jnp.concatenate([jnp.cos(angle), jnp.sin(angle)], axis=-1)


def sigma_of(steps_now):
    unit_time = steps_now.astype(jnp.float32) / 1000.0
    return 5.0 * unit_time / (1.0 + 4.0 * unit_time)


def attend(exchanged):
    items = exchanged.shape[0]
    length = exchanged.shape[1]
    local_heads = exchanged.shape[2]
    query_all = exchanged[..., :HEAD]
    key_rows = exchanged[..., HEAD : 2 * HEAD]
    value_rows = exchanged[..., 2 * HEAD :]
    block_rows = min(512, length)
    block_count = length // block_rows

    def one_block(block_index):
        query_block = lax.dynamic_slice_in_dim(query_all, block_index * block_rows, block_rows, 1)
        scores = jnp.einsum(
            "nqhe,nkhe->nhqk", query_block, key_rows, preferred_element_type=jnp.float32
        ) * HEAD ** (-0.5)
        row_max = jnp.max(scores, axis=-1, keepdims=True)
        exp_scores = jnp.exp(scores - row_max)
        row_sum = jnp.sum(exp_scores, axis=-1, keepdims=True)
        weights = (exp_scores / row_sum).astype(jnp.bfloat16)
        return jnp.einsum(
            "nhqk,nkhe->nqhe", weights, value_rows, preferred_element_type=jnp.float32
        ).astype(jnp.bfloat16)

    blocks = lax.map(one_block, jnp.arange(block_count, dtype=jnp.int32))
    return blocks.transpose(1, 0, 2, 3, 4).reshape(items, length, local_heads * HEAD)


def body(head_inputs, hidden, out_weight, time_weight, head_weight, latent, timesteps):
    samples = head_inputs.shape[1]
    row_count = head_inputs.shape[2]
    flat_count = samples * row_count
    local = head_inputs.reshape(samples, row_count, HEADS, 3 * HEAD)
    attended = lax.all_to_all(
        attend(lax.all_to_all(local, "seq", split_axis=2, concat_axis=1, tiled=True)),
        "seq",
        split_axis=1,
        concat_axis=2,
        tiled=True,
    )
    flattened = attended.reshape(flat_count, HEADS * HEAD)
    time_full, head_full = (
        lax.all_gather(time_weight, ("seq", "fsdp"), axis=2, tiled=True),
        lax.all_gather(head_weight, ("seq", "fsdp"), axis=1, tiled=True),
    )
    embedding = time_embed(timesteps[0, :, 0]).astype(jnp.bfloat16)
    modulation = jnp.dot(embedding, time_full[0], preferred_element_type=jnp.float32)
    gate_term = modulation[:, None, :DIM]
    shift_term = modulation[:, None, DIM : 2 * DIM]
    scale_term = modulation[:, None, 2 * DIM :]
    own_columns = lax.all_to_all(flattened, "fsdp", split_axis=1, concat_axis=0, tiled=True)
    projected = lax.psum_scatter(
        jnp.dot(own_columns, out_weight[0], preferred_element_type=jnp.float32).astype(
            jnp.bfloat16
        ),
        "fsdp",
        scatter_dimension=0,
        tiled=True,
    ).astype(jnp.float32)
    updated = hidden.reshape(samples, row_count, DIM).astype(
        jnp.float32
    ) + gate_term * projected.reshape(samples, row_count, DIM)
    average = jnp.mean(updated, axis=-1, keepdims=True)
    centred = updated - average
    variance = jnp.mean(centred * centred, axis=-1, keepdims=True)
    normed = (centred * lax.rsqrt(variance + 1e-06) * (1.0 + scale_term) + shift_term).astype(
        jnp.bfloat16
    )
    velocity = jnp.dot(
        normed.reshape(flat_count, DIM), head_full[0], preferred_element_type=jnp.float32
    )
    velocity = velocity.reshape(1, samples, row_count // 2, 2 * PATCH)
    step_size = sigma_of(timesteps[0, :, 1]) - sigma_of(timesteps[0, :, 0])
    stepped = latent + step_size[None, :, None, None] * velocity
    carried = partner(stepped, "section", 0)
    return (velocity, carried)


MESH = pl.DeviceIdType.MESH
BF16 = jnp.bfloat16
F32 = jnp.float32


def up(value, step):
    return -(-value // step) * step


class Plan:
    def __init__(self, seq, fsdp, rows):
        self.seq, self.fsdp, self.rows = seq, fsdp, rows
        self.heads = HEADS // seq
        self.group_in = self.heads * 3 * HEAD
        self.group_out = self.heads * HEAD
        per = max(1, self.heads // 4)
        marks = sorted({*range(0, self.heads + 1, per), self.heads - 1, self.heads})
        self.chunks = []
        lo_in = lo_out = 0
        for first, last in zip(marks, marks[1:]):
            hi_in = min(up(last * 3 * HEAD, 128), self.group_in)
            hi_out = last * HEAD // 128 * 128 if last < self.heads else self.group_out
            self.chunks.append((first, last, (lo_in, hi_in), (lo_out, hi_out)))
            lo_in, lo_out = hi_in, hi_out
        self.block = 512
        self.blocks = DIM // self.block


def fused(
    plan, qkv, hid, ow, tw, hw, lat, ts, freqs, vel_out, car_out,
    qkv_v, ow_v, tw_v, hid_v, lat_v, emb, mod_loc, mod_all, att, gath, own, part, got, packed, head_v,
    upd, vel_v, step_v, step_in,
    loc_sem, own_sem, qs, qr, es, er, ms, mr, hxs, hxr, hzs, hzr, as_, ar, ps, pr, cs, cr,
):
    seq, fsdp, rows = plan.seq, plan.fsdp, plan.rows
    z, f, s = lax.axis_index("seq"), lax.axis_index("fsdp"), lax.axis_index("section")
    other = 1 - f
    slot = z * fsdp + f
    per_half = seq // fsdp
    n_chunks = len(plan.chunks)

    def remote(src, dst, send, recv, to):
        return pltpu.make_async_remote_copy(
            src_ref=src, dst_ref=dst, send_sem=send, recv_sem=recv, device_id=to, device_id_type=MESH
        )

    barrier = pltpu.get_barrier_semaphore()
    for dz in range(seq):
        for df in range(fsdp):
            if dz or df:
                to = {"seq": z ^ dz, "fsdp": f ^ df}
                pl.semaphore_signal(barrier, inc=1, device_id=to, device_id_type=MESH)
    pl.semaphore_signal(barrier, inc=1, device_id={"section": 1 - s}, device_id_type=MESH)

    loads = [
        pltpu.make_async_copy(hw.at[0], packed.at[slot], loc_sem.at[0]),
        pltpu.make_async_copy(tw.at[0], tw_v, loc_sem.at[1]),
        pltpu.make_async_copy(ow.at[0], ow_v, loc_sem.at[2]),
        pltpu.make_async_copy(hid.at[0, 0], hid_v, loc_sem.at[3]),
        pltpu.make_async_copy(lat.at[0, 0], lat_v, loc_sem.at[4]),
    ]

    def group_of(position):
        return lax.rem(position, fsdp) * per_half + position // fsdp

    def columns(position, span):
        first = group_of(position) * plan.group_in + span[0]
        return pl.ds(pl.multiple_of(first, 128), span[1] - span[0])

    def my_rows(position):
        return pl.ds(pl.multiple_of(position * rows, rows), rows)

    own_loads = []
    for c, (_, _, span, _) in enumerate(plan.chunks):
        own_loads.append(
            pltpu.make_async_copy(
                qkv.at[0, 0, :, columns(z, span)],
                qkv_v.at[my_rows(z), span[0] : span[1]],
                own_sem.at[c],
            )
        )
        own_loads[-1].start()
    for load in loads:
        load.start()

    t_now = ts[0, 0, 0].astype(F32)
    angle = t_now * jnp.broadcast_to(freqs[...], (8, FREQ // 2))
    emb[f, :, : FREQ // 2] = jnp.cos(angle)
    emb[f, :, FREQ // 2 :] = jnp.sin(angle)

    pl.semaphore_wait(barrier, seq * fsdp)

    order = sorted(range(1, seq), reverse=True)
    sends = []
    emb_copy = remote(emb.at[f], emb.at[f], es, er, {"fsdp": other})
    emb_copy.start()
    in_copies = []
    for c, (_, _, span, _) in enumerate(plan.chunks):
        row = []
        for d in order:
            peer = z ^ d
            row.append(
                remote(
                    qkv.at[0, 0, :, columns(peer, span)],
                    qkv_v.at[my_rows(z), span[0] : span[1]],
                    qs.at[c, d],
                    qr.at[c, d],
                    {"seq": peer},
                )
            )
            row[-1].start()
        in_copies.append(row)

    loads[0].wait()
    head_copy = remote(packed.at[slot], packed.at[slot], hxs, hxr, {"fsdp": other})
    head_copy.start()

    emb_copy.wait()
    loads[1].wait()
    both = emb[...].reshape(fsdp * 8, FREQ).astype(BF16)
    mod = lax.dot_general(both, tw_v[...], (((1,), (1,)), ((), ())), preferred_element_type=F32)
    for b in range(fsdp):
        mod_loc[b] = mod[b * 8 : b * 8 + 1]
    mod_all[slot] = mod_loc[f]
    mod_copies = []
    for dz in range(seq):
        for df in range(fsdp):
            if dz or df:
                mod_copies.append(
                    remote(
                        mod_loc.at[f ^ df],
                        mod_all.at[slot],
                        ms.at[dz, df],
                        mr.at[dz, df],
                        {"seq": z ^ dz, "fsdp": f ^ df},
                    )
                )
                mod_copies[-1].start()

    half = lax.rem(z, fsdp)
    part_of_half = z // fsdp
    for c, (first, last, _, span) in enumerate(plan.chunks):
        own_loads[c].wait()
        for copy in in_copies[c]:
            copy.wait_recv()
        for h in range(first, last):
            base = h * 3 * HEAD
            query = qkv_v[:, base : base + HEAD]
            key = qkv_v[:, base + HEAD : base + 2 * HEAD]
            value = qkv_v[:, base + 2 * HEAD : base + 3 * HEAD]
            scores = lax.dot_general(
                query, key, (((1,), (1,)), ((), ())), preferred_element_type=F32
            ) * HEAD ** (-0.5)
            exps = jnp.exp(scores - jnp.max(scores, axis=-1, keepdims=True))
            weights = (exps * (1.0 / jnp.sum(exps, axis=-1, keepdims=True))).astype(BF16)
            att[:, h * HEAD : (h + 1) * HEAD] = jnp.dot(
                weights, value, preferred_element_type=F32
            ).astype(BF16)
        lo, hi = span
        for d in [*order, 0]:
            peer = z ^ d
            source = att.at[my_rows(peer), lo:hi]
            target = gath.at[f, part_of_half, :, lo:hi]
            if d:
                remote(
                    source, target, as_.at[c, d], ar.at[c, f, part_of_half], {"seq": peer, "fsdp": half}
                ).start()
            else:

                @pl.when(half == f)
                def _():
                    pltpu.make_async_copy(source, target, ar.at[c, f, part_of_half]).start()

                @pl.when(half != f)
                def _():
                    remote(
                        source, target, as_.at[c, d], ar.at[c, f, part_of_half], {"fsdp": half}
                    ).start()

    def arrive(c):
        lo, hi = plan.chunks[c][3]
        for b in range(fsdp):
            for i in range(per_half):
                block = gath.at[b, i, :, lo:hi]
                pltpu.make_async_copy(block, block, ar.at[c, b, i]).wait()

    def tokens(i, lo, hi):
        return gath[:, i, :, lo:hi].reshape(fsdp * rows, hi - lo)

    def weights_of(i, lo, hi, cols):
        return ow_v[i * plan.group_out + lo : i * plan.group_out + hi, cols]

    loads[2].wait()
    late = plan.chunks[-1][3][0]
    for c in range(n_chunks - 1):
        arrive(c)
    blocks = [slice(k * plan.block, (k + 1) * plan.block) for k in range(plan.blocks)]
    for cols in blocks:
        total = jnp.zeros((fsdp * rows, plan.block), F32)
        for i in range(per_half):
            total += jnp.dot(
                tokens(i, 0, late), weights_of(i, 0, late, cols), preferred_element_type=F32
            )
        for b in range(fsdp):
            own[b, :, cols] = total[b * rows : (b + 1) * rows]
    arrive(n_chunks - 1)
    last_tokens = jnp.concatenate(
        [tokens(i, late, plan.group_out) for i in range(per_half)], axis=1
    )
    part_copies = []
    for k, cols in enumerate(blocks):
        last_weights = jnp.concatenate(
            [weights_of(i, late, plan.group_out, cols) for i in range(per_half)], axis=0
        )
        total = jnp.dot(last_tokens, last_weights, preferred_element_type=F32)
        for b in range(fsdp):
            projected = own[b, :, cols] + total[b * rows : (b + 1) * rows]
            own[b, :, cols] = projected
            part[b, :, cols] = projected.astype(BF16)
        part_copies.append(
            remote(part.at[other, :, cols], got.at[:, cols], ps.at[k], pr.at[k], {"fsdp": other})
        )
        part_copies[-1].start()

    head_copy.wait()
    head_copies = []
    for d in order:
        for b, index in enumerate((slot, z * fsdp + other)):
            head_copies.append(
                remote(packed.at[index], packed.at[index], hzs.at[b, d], hzr.at[b, d], {"seq": z ^ d})
            )
            head_copies[-1].start()

    for copy in mod_copies:
        copy.wait_recv()
    modulation = jnp.concatenate([mod_all[j] for j in range(seq * fsdp)], axis=1)
    gate = modulation[:, :DIM]
    shift = modulation[:, DIM : 2 * DIM]
    scale = modulation[:, 2 * DIM :]
    loads[3].wait()
    loads[4].wait()

    means, squares = [], []
    for k, cols in enumerate(blocks):
        part_copies[k].wait_recv()
        projected = own[f, :, cols] + got[:, cols].astype(F32)
        now = hid_v[:, cols].astype(F32) + gate[:, cols] * projected
        upd[:, cols] = now
        mean = jnp.mean(now, axis=-1, keepdims=True)
        means.append(mean)
        squares.append(jnp.sum((now - mean) * (now - mean), axis=-1, keepdims=True))
    average = sum(means) * (1.0 / plan.blocks)
    spread = sum((mean - average) * (mean - average) for mean in means) * plan.block
    variance = (sum(squares) + spread) * (1.0 / DIM)
    for copy in head_copies:
        copy.wait_recv()
    head_full = jnp.concatenate([packed[j] for j in range(seq * fsdp)], axis=1)
    head_v[:PATCH] = head_full
    head_v[PATCH:] = head_full
    normed = (
        (upd[...] - average) * lax.rsqrt(variance + 1e-06) * (1.0 + scale) + shift
    ).astype(BF16)
    vel_v[...] = lax.dot_general(
        normed, head_v[...], (((1,), (1,)), ((), ())), preferred_element_type=F32
    )
    even = vel_v[pl.ds(0, rows // 2, 2), :]
    odd = vel_v[pl.ds(1, rows // 2, 2), :]
    left = lax.broadcasted_iota(jnp.int32, even.shape, 1) < PATCH
    velocity = jnp.where(left, even, odd)
    vel_out[0, 0] = velocity

    unit = jnp.full((1, 2 * PATCH), ts[0, 0, 0].astype(F32), F32) / 1000.0
    unit_next = jnp.full((1, 2 * PATCH), ts[0, 0, 1].astype(F32), F32) / 1000.0
    step = 5.0 * unit_next / (1.0 + 4.0 * unit_next) - 5.0 * unit / (1.0 + 4.0 * unit)
    step_v[...] = lat_v[...] + step * velocity
    swap = remote(step_v, step_in, cs, cr, {"section": 1 - s})
    swap.start()

    for row in in_copies:
        for copy in row:
            copy.wait_send()
    for copy in mod_copies + head_copies + part_copies:
        copy.wait_send()
    for c, (_, _, _, (lo, hi)) in enumerate(plan.chunks):
        for d in order:
            block = att.at[0:rows, lo:hi]
            pltpu.make_async_copy(block, block, as_.at[c, d]).wait()

        @pl.when(half != f)
        def _():
            block = att.at[0:rows, lo:hi]
            pltpu.make_async_copy(block, block, as_.at[c, 0]).wait()

    swap.wait()
    car_out[0, 0] = step_in[...]


def fused_body(plan, head_inputs, hidden, out_weight, time_weight, head_weight, latent, timesteps):
    seq, fsdp, rows = plan.seq, plan.fsdp, plan.rows
    chunks = len(plan.chunks)
    time_weight, head_weight = time_weight.swapaxes(1, 2), head_weight.swapaxes(1, 2)
    per_half = seq // fsdp
    half = FREQ // 2
    freqs = np.exp(-math.log(10000.0) * np.arange(half) / half).astype(np.float32)[None]
    dma = pltpu.SemaphoreType.DMA
    vmem = pltpu.VMEM
    whole = pl.BlockSpec(memory_space=pltpu.VMEM)
    anywhere = pl.BlockSpec(memory_space=pltpu.HBM)
    parts = seq * fsdp
    return pl.pallas_call(
        functools.partial(fused, plan),
        out_shape=(
            jax.ShapeDtypeStruct(latent.shape, F32),
            jax.ShapeDtypeStruct(latent.shape, F32),
        ),
        in_specs=[anywhere] * 6 + [pl.BlockSpec(memory_space=pltpu.SMEM), whole],
        out_specs=(whole, whole),
        scratch_shapes=[
            vmem((seq * rows, plan.group_in), BF16),
            vmem(out_weight.shape[1:], BF16),
            vmem(time_weight.shape[1:], BF16),
            vmem((rows, DIM), BF16),
            vmem(latent.shape[2:], F32),
            vmem((fsdp, 8, FREQ), F32),
            vmem((fsdp, 1, time_weight.shape[1]), F32),
            vmem((parts, 1, time_weight.shape[1]), F32),
            vmem((seq * rows, plan.group_out), BF16),
            vmem((fsdp, per_half, rows, plan.group_out), BF16),
            vmem((fsdp, rows, DIM), F32),
            vmem((fsdp, rows, DIM), BF16),
            vmem((rows, DIM), BF16),
            vmem((parts, *head_weight.shape[1:]), BF16),
            vmem((2 * PATCH, DIM), BF16),
            vmem((rows, DIM), F32),
            vmem((rows, 2 * PATCH), F32),
            vmem(latent.shape[2:], F32),
            vmem(latent.shape[2:], F32),
            dma((5,)),
            dma((chunks,)),
            dma((chunks, seq)),
            dma((chunks, seq)),
            dma,
            dma,
            dma((seq, fsdp)),
            dma((seq, fsdp)),
            dma,
            dma,
            dma((fsdp, seq)),
            dma((fsdp, seq)),
            dma((chunks, seq)),
            dma((chunks, fsdp, per_half)),
            dma((plan.blocks,)),
            dma((plan.blocks,)),
            dma,
            dma,
        ],
        compiler_params=pltpu.CompilerParams(
            collective_id=0, has_side_effects=True, vmem_limit_bytes=58 * 2**20
        ),
        name="fused_step",
    )(head_inputs, hidden, out_weight, time_weight, head_weight, latent, timesteps, freqs)


def pick(mesh):
    seq, fsdp, sections = mesh.shape["seq"], mesh.shape["fsdp"], mesh.shape["section"]

    def run(*blocks):
        samples, rows = blocks[0].shape[1:3]
        fits = (
            samples == 1
            and fsdp == 2
            and sections == 2
            and seq & (seq - 1) == 0
            and seq % fsdp == 0
            and HEADS % seq == 0
            and (HEADS // seq * HEAD) % 128 == 0
            and rows % 16 == 0
            and seq * rows <= 512
            and DIM % 512 == 0
        )
        if fits:
            return fused_body(Plan(seq, fsdp, rows), *blocks)
        return body(*blocks)

    return run


def solution(mesh):
    return jax.shard_map(
        pick(mesh),
        mesh=mesh,
        in_specs=(
            P("section", ("grp", "fsdp"), "seq", None),
            P("section", ("grp", "fsdp"), "seq", None),
            P("section", "fsdp", None),
            P("section", None, ("seq", "fsdp")),
            P("section", ("seq", "fsdp"), None),
            P("section", ("grp", "fsdp"), "seq", None),
            P("section", ("grp", "fsdp"), None),
        ),
        out_specs=(
            P("section", ("grp", "fsdp"), "seq", None),
            P("section", ("grp", "fsdp"), "seq", None),
        ),
        check_vma=False,
    )
```

```python
import functools
import math

import jax
import jax.numpy as jnp
import numpy as np
from jax import lax
from jax.experimental import pallas as pl
from jax.experimental.pallas import tpu as pltpu
from jax.sharding import PartitionSpec as P

DIM = 2560
HEADS = 32
HEAD = 80
PATCH = 64
FREQ = 256


def partner(block, axis, apart):
    count = lax.axis_size(axis)
    route = []
    for low in range(count):
        high = low | 1 << apart
        if high != low and high < count:
            route += [(low, high), (high, low)]
    return lax.ppermute(block, axis, route)


def time_embed(steps_now):
    half = FREQ // 2
    freqs = jnp.exp(-math.log(10000.0) * jnp.arange(half, dtype=jnp.float32) / half)
    angle = steps_now.astype(jnp.float32)[..., None] * freqs
    return jnp.concatenate([jnp.cos(angle), jnp.sin(angle)], axis=-1)


def sigma_of(steps_now):
    unit_time = steps_now.astype(jnp.float32) / 1000.0
    return 5.0 * unit_time / (1.0 + 4.0 * unit_time)


def attend(exchanged):
    items = exchanged.shape[0]
    length = exchanged.shape[1]
    local_heads = exchanged.shape[2]
    query_all = exchanged[..., :HEAD]
    key_rows = exchanged[..., HEAD : 2 * HEAD]
    value_rows = exchanged[..., 2 * HEAD :]
    block_rows = min(512, length)
    block_count = length // block_rows

    def one_block(block_index):
        query_block = lax.dynamic_slice_in_dim(query_all, block_index * block_rows, block_rows, 1)
        scores = jnp.einsum(
            "nqhe,nkhe->nhqk", query_block, key_rows, preferred_element_type=jnp.float32
        ) * HEAD ** (-0.5)
        row_max = jnp.max(scores, axis=-1, keepdims=True)
        exp_scores = jnp.exp(scores - row_max)
        row_sum = jnp.sum(exp_scores, axis=-1, keepdims=True)
        weights = (exp_scores / row_sum).astype(jnp.bfloat16)
        return jnp.einsum(
            "nhqk,nkhe->nqhe", weights, value_rows, preferred_element_type=jnp.float32
        ).astype(jnp.bfloat16)

    blocks = lax.map(one_block, jnp.arange(block_count, dtype=jnp.int32))
    return blocks.transpose(1, 0, 2, 3, 4).reshape(items, length, local_heads * HEAD)


def body(head_inputs, hidden, out_weight, time_weight, head_weight, latent, timesteps):
    samples = head_inputs.shape[1]
    row_count = head_inputs.shape[2]
    flat_count = samples * row_count
    local = head_inputs.reshape(samples, row_count, HEADS, 3 * HEAD)
    attended = lax.all_to_all(
        attend(lax.all_to_all(local, "seq", split_axis=2, concat_axis=1, tiled=True)),
        "seq",
        split_axis=1,
        concat_axis=2,
        tiled=True,
    )
    flattened = attended.reshape(flat_count, HEADS * HEAD)
    time_full, head_full = (
        lax.all_gather(time_weight, ("seq", "fsdp"), axis=2, tiled=True),
        lax.all_gather(head_weight, ("seq", "fsdp"), axis=1, tiled=True),
    )
    embedding = time_embed(timesteps[0, :, 0]).astype(jnp.bfloat16)
    modulation = jnp.dot(embedding, time_full[0], preferred_element_type=jnp.float32)
    gate_term = modulation[:, None, :DIM]
    shift_term = modulation[:, None, DIM : 2 * DIM]
    scale_term = modulation[:, None, 2 * DIM :]
    own_columns = lax.all_to_all(flattened, "fsdp", split_axis=1, concat_axis=0, tiled=True)
    projected = lax.psum_scatter(
        jnp.dot(own_columns, out_weight[0], preferred_element_type=jnp.float32).astype(
            jnp.bfloat16
        ),
        "fsdp",
        scatter_dimension=0,
        tiled=True,
    ).astype(jnp.float32)
    updated = hidden.reshape(samples, row_count, DIM).astype(
        jnp.float32
    ) + gate_term * projected.reshape(samples, row_count, DIM)
    average = jnp.mean(updated, axis=-1, keepdims=True)
    centred = updated - average
    variance = jnp.mean(centred * centred, axis=-1, keepdims=True)
    normed = (centred * lax.rsqrt(variance + 1e-06) * (1.0 + scale_term) + shift_term).astype(
        jnp.bfloat16
    )
    velocity = jnp.dot(
        normed.reshape(flat_count, DIM), head_full[0], preferred_element_type=jnp.float32
    )
    velocity = velocity.reshape(1, samples, row_count // 2, 2 * PATCH)
    step_size = sigma_of(timesteps[0, :, 1]) - sigma_of(timesteps[0, :, 0])
    stepped = latent + step_size[None, :, None, None] * velocity
    carried = partner(stepped, "section", 0)
    return (velocity, carried)


MESH = pl.DeviceIdType.MESH
BF16 = jnp.bfloat16
F32 = jnp.float32


def up(value, step):
    return -(-value // step) * step


class Plan:
    def __init__(self, seq, fsdp, rows):
        self.seq, self.fsdp, self.rows = seq, fsdp, rows
        self.heads = HEADS // seq
        self.group_in = self.heads * 3 * HEAD
        self.group_out = self.heads * HEAD
        per = max(1, self.heads // 4)
        marks = sorted({*range(0, self.heads + 1, per), self.heads - 1, self.heads})
        self.chunks = []
        lo_in = lo_out = 0
        for first, last in zip(marks, marks[1:]):
            hi_in = min(up(last * 3 * HEAD, 128), self.group_in)
            hi_out = last * HEAD // 128 * 128 if last < self.heads else self.group_out
            self.chunks.append((first, last, (lo_in, hi_in), (lo_out, hi_out)))
            lo_in, lo_out = hi_in, hi_out
        self.block = 512
        self.blocks = DIM // self.block


def fused(
    plan, qkv, hid, ow, tw, hw, lat, ts, freqs, out,
    qkv_v, ow_v, tw_v, hid_v, lat_v, emb, mod_loc, mod_all, att, gath, own, part, got, packed, head_v,
    upd, vel_v, step_v, step_in,
    loc_sem, own_sem, qs, qr, es, er, ms, mr, hxs, hxr, hzs, hzr, gs, gr, as_, ar, ps, pr, cs, cr,
):
    seq, fsdp, rows = plan.seq, plan.fsdp, plan.rows
    z, f, s = lax.axis_index("seq"), lax.axis_index("fsdp"), lax.axis_index("section")
    g = lax.axis_index("grp")
    other = 1 - f
    slot = z * fsdp + f
    per_half = seq // fsdp
    n_chunks = len(plan.chunks)

    def remote(src, dst, send, recv, to):
        return pltpu.make_async_remote_copy(
            src_ref=src, dst_ref=dst, send_sem=send, recv_sem=recv, device_id=to, device_id_type=MESH
        )

    barrier = pltpu.get_barrier_semaphore()
    for dz in range(seq):
        for df in range(fsdp):
            if dz or df:
                to = {"seq": z ^ dz, "fsdp": f ^ df}
                pl.semaphore_signal(barrier, inc=1, device_id=to, device_id_type=MESH)
    pl.semaphore_signal(barrier, inc=1, device_id={"section": 1 - s}, device_id_type=MESH)
    pl.semaphore_signal(barrier, inc=1, device_id={"grp": 1 - g}, device_id_type=MESH)

    loads = [
        pltpu.make_async_copy(hw.at[0], packed.at[slot], loc_sem.at[0]),
        pltpu.make_async_copy(tw.at[0], tw_v, loc_sem.at[1]),
        pltpu.make_async_copy(ow.at[0], ow_v, loc_sem.at[2]),
        pltpu.make_async_copy(hid.at[0, 0], hid_v, loc_sem.at[3]),
        pltpu.make_async_copy(lat.at[0, 0], lat_v, loc_sem.at[4]),
    ]

    def group_of(position):
        return lax.rem(position, fsdp) * per_half + position // fsdp

    def columns(position, span):
        first = group_of(position) * plan.group_in + span[0]
        return pl.ds(pl.multiple_of(first, 128), span[1] - span[0])

    def my_rows(position):
        return pl.ds(pl.multiple_of(position * rows, rows), rows)

    own_loads = []
    for c, (_, _, span, _) in enumerate(plan.chunks):
        own_loads.append(
            pltpu.make_async_copy(
                qkv.at[0, 0, :, columns(z, span)],
                qkv_v.at[my_rows(z), span[0] : span[1]],
                own_sem.at[c],
            )
        )
        own_loads[-1].start()
    for load in loads:
        load.start()

    pl.semaphore_wait(barrier, seq * fsdp + 1)

    order = sorted(range(1, seq), reverse=True)
    sends = []
    in_copies = []
    for c, (_, _, span, _) in enumerate(plan.chunks):
        row = []
        for d in order:
            peer = z ^ d
            row.append(
                remote(
                    qkv.at[0, 0, :, columns(peer, span)],
                    qkv_v.at[my_rows(z), span[0] : span[1]],
                    qs.at[c, d],
                    qr.at[c, d],
                    {"seq": peer},
                )
            )
            row[-1].start()
        in_copies.append(row)

    t_now = ts[0, 0, 0].astype(F32)
    angle = t_now * jnp.broadcast_to(freqs[...], (8, FREQ // 2))
    emb[f, :, : FREQ // 2] = jnp.cos(angle)
    emb[f, :, FREQ // 2 :] = jnp.sin(angle)

    emb_copy = remote(emb.at[f], emb.at[f], es, er, {"fsdp": other})
    emb_copy.start()

    loads[0].wait()
    head_copy = remote(packed.at[slot], packed.at[slot], hxs, hxr, {"fsdp": other})
    head_copy.start()

    emb_copy.wait()
    loads[1].wait()
    both = emb[...].reshape(fsdp * 8, FREQ).astype(BF16)
    mod = lax.dot_general(both, tw_v[...], (((1,), (1,)), ((), ())), preferred_element_type=F32)
    for b in range(fsdp):
        mod_loc[b] = mod[b * 8 : b * 8 + 1]
    mod_all[slot] = mod_loc[f]
    mod_copies = []
    for dz in range(seq):
        for df in range(fsdp):
            if dz or df:
                mod_copies.append(
                    remote(
                        mod_loc.at[f ^ df],
                        mod_all.at[slot],
                        ms.at[dz, df],
                        mr.at[dz, df],
                        {"seq": z ^ dz, "fsdp": f ^ df},
                    )
                )
                mod_copies[-1].start()

    half = lax.rem(z, fsdp)
    part_of_half = z // fsdp
    for c, (first, last, _, span) in enumerate(plan.chunks):
        own_loads[c].wait()
        for copy in in_copies[c]:
            copy.wait_recv()
        for h in range(first, last):
            base = h * 3 * HEAD
            query = qkv_v[:, base : base + HEAD]
            key = qkv_v[:, base + HEAD : base + 2 * HEAD]
            value = qkv_v[:, base + 2 * HEAD : base + 3 * HEAD]
            scores = lax.dot_general(
                query, key, (((1,), (1,)), ((), ())), preferred_element_type=F32
            ) * HEAD ** (-0.5)
            exps = jnp.exp(scores - jnp.max(scores, axis=-1, keepdims=True))
            weights = (exps * (1.0 / jnp.sum(exps, axis=-1, keepdims=True))).astype(BF16)
            att[:, h * HEAD : (h + 1) * HEAD] = jnp.dot(
                weights, value, preferred_element_type=F32
            ).astype(BF16)
        lo, hi = span
        for d in [*order, 0]:
            peer = z ^ d
            source = att.at[my_rows(peer), lo:hi]
            target = gath.at[f, part_of_half, :, lo:hi]
            if d:
                remote(
                    source, target, as_.at[c, d], ar.at[c, f, part_of_half], {"seq": peer, "fsdp": half}
                ).start()
            else:

                @pl.when(half == f)
                def _():
                    pltpu.make_async_copy(source, target, ar.at[c, f, part_of_half]).start()

                @pl.when(half != f)
                def _():
                    remote(
                        source, target, as_.at[c, d], ar.at[c, f, part_of_half], {"fsdp": half}
                    ).start()

    def arrive(c):
        lo, hi = plan.chunks[c][3]
        for b in range(fsdp):
            for i in range(per_half):
                block = gath.at[b, i, :, lo:hi]
                pltpu.make_async_copy(block, block, ar.at[c, b, i]).wait()

    def tokens(i, lo, hi):
        return gath[:, i, :, lo:hi].reshape(fsdp * rows, hi - lo)

    def weights_of(i, lo, hi, cols):
        return ow_v[i * plan.group_out + lo : i * plan.group_out + hi, cols]

    loads[2].wait()
    late = plan.chunks[-1][3][0]
    for c in range(n_chunks - 1):
        arrive(c)
    blocks = [slice(k * plan.block, (k + 1) * plan.block) for k in range(plan.blocks)]
    for cols in blocks:
        total = jnp.zeros((fsdp * rows, plan.block), F32)
        for i in range(per_half):
            total += jnp.dot(
                tokens(i, 0, late), weights_of(i, 0, late, cols), preferred_element_type=F32
            )
        for b in range(fsdp):
            own[b, :, cols] = total[b * rows : (b + 1) * rows]
    arrive(n_chunks - 1)
    head_copy.wait()
    head_copies = []
    half_rows = PATCH // 2
    my_half = pl.ds(pl.multiple_of(g * half_rows, half_rows), half_rows)
    for d in order:
        for b, column in enumerate((f, other)):
            source = packed.at[z * fsdp + column, my_half]
            head_copies.append(
                (
                    remote(source, source, hzs.at[b, d], hzr.at[b, d], {"seq": z ^ d}),
                    (z ^ d) * fsdp + column,
                )
            )
            head_copies[-1][0].start()
    last_tokens = jnp.concatenate(
        [tokens(i, late, plan.group_out) for i in range(per_half)], axis=1
    )
    part_copies = []
    for k, cols in enumerate(blocks):
        last_weights = jnp.concatenate(
            [weights_of(i, late, plan.group_out, cols) for i in range(per_half)], axis=0
        )
        total = jnp.dot(last_tokens, last_weights, preferred_element_type=F32)
        for b in range(fsdp):
            projected = own[b, :, cols] + total[b * rows : (b + 1) * rows]
            own[b, :, cols] = projected
            part[b, :, cols] = projected.astype(BF16)
        part_copies.append(
            remote(part.at[other, :, cols], got.at[:, cols], ps.at[k], pr.at[k], {"fsdp": other})
        )
        part_copies[-1].start()

    pass_copies = []
    for copy, index in head_copies:
        copy.wait_recv()
        source = packed.at[index, my_half]
        pass_copies.append(
            remote(source, source, gs.at[len(pass_copies)], gr.at[len(pass_copies)], {"grp": 1 - g})
        )
        pass_copies[-1].start()

    for copy in mod_copies:
        copy.wait_recv()
    modulation = jnp.concatenate([mod_all[j] for j in range(seq * fsdp)], axis=1)
    gate = modulation[:, :DIM]
    shift = modulation[:, DIM : 2 * DIM]
    scale = modulation[:, 2 * DIM :]
    loads[3].wait()
    loads[4].wait()

    means, squares = [], []
    for k, cols in enumerate(blocks):
        part_copies[k].wait_recv()
        projected = own[f, :, cols] + got[:, cols].astype(F32)
        now = hid_v[:, cols].astype(F32) + gate[:, cols] * projected
        upd[:, cols] = now
        mean = jnp.mean(now, axis=-1, keepdims=True)
        means.append(mean)
        squares.append(jnp.sum((now - mean) * (now - mean), axis=-1, keepdims=True))
    average = sum(means) * (1.0 / plan.blocks)
    spread = sum((mean - average) * (mean - average) for mean in means) * plan.block
    variance = (sum(squares) + spread) * (1.0 / DIM)
    for copy in pass_copies:
        copy.wait_recv()
    head_full = jnp.concatenate([packed[j] for j in range(seq * fsdp)], axis=1)
    head_v[:PATCH] = head_full
    head_v[PATCH:] = head_full
    normed = (
        (upd[...] - average) * lax.rsqrt(variance + 1e-06) * (1.0 + scale) + shift
    ).astype(BF16)
    vel_v[...] = lax.dot_general(
        normed, head_v[...], (((1,), (1,)), ((), ())), preferred_element_type=F32
    )
    even = vel_v[pl.ds(0, rows // 2, 2), :]
    odd = vel_v[pl.ds(1, rows // 2, 2), :]
    left = lax.broadcasted_iota(jnp.int32, even.shape, 1) < PATCH
    velocity = jnp.where(left, even, odd)
    out[0] = velocity

    unit = jnp.full((1, 2 * PATCH), ts[0, 0, 0].astype(F32), F32) / 1000.0
    unit_next = jnp.full((1, 2 * PATCH), ts[0, 0, 1].astype(F32), F32) / 1000.0
    step = 5.0 * unit_next / (1.0 + 4.0 * unit_next) - 5.0 * unit / (1.0 + 4.0 * unit)
    step_v[...] = lat_v[...] + step * velocity
    swap = remote(step_v, step_in, cs, cr, {"section": 1 - s})
    swap.start()

    for row in in_copies:
        for copy in row:
            copy.wait_send()
    for copy in mod_copies + [copy for copy, _ in head_copies] + pass_copies + part_copies:
        copy.wait_send()
    for c, (_, _, _, (lo, hi)) in enumerate(plan.chunks):
        for d in order:
            block = att.at[0:rows, lo:hi]
            pltpu.make_async_copy(block, block, as_.at[c, d]).wait()

        @pl.when(half != f)
        def _():
            block = att.at[0:rows, lo:hi]
            pltpu.make_async_copy(block, block, as_.at[c, 0]).wait()

    swap.wait()
    out[1] = step_in[...]


def fused_body(plan, head_inputs, hidden, out_weight, time_weight, head_weight, latent, timesteps):
    seq, fsdp, rows = plan.seq, plan.fsdp, plan.rows
    chunks = len(plan.chunks)
    time_weight, head_weight = time_weight.swapaxes(1, 2), head_weight.swapaxes(1, 2)
    per_half = seq // fsdp
    half = FREQ // 2
    freqs = np.exp(-math.log(10000.0) * np.arange(half) / half).astype(np.float32)[None]
    dma = pltpu.SemaphoreType.DMA
    vmem = pltpu.VMEM
    whole = pl.BlockSpec(memory_space=pltpu.VMEM)
    anywhere = pl.BlockSpec(memory_space=pltpu.HBM)
    parts = seq * fsdp
    out = pl.pallas_call(
        functools.partial(fused, plan),
        out_shape=jax.ShapeDtypeStruct((2, *latent.shape[2:]), F32),
        in_specs=[anywhere] * 6 + [pl.BlockSpec(memory_space=pltpu.SMEM), whole],
        out_specs=whole,
        scratch_shapes=[
            vmem((seq * rows, plan.group_in), BF16),
            vmem(out_weight.shape[1:], BF16),
            vmem(time_weight.shape[1:], BF16),
            vmem((rows, DIM), BF16),
            vmem(latent.shape[2:], F32),
            vmem((fsdp, 8, FREQ), F32),
            vmem((fsdp, 1, time_weight.shape[1]), F32),
            vmem((parts, 1, time_weight.shape[1]), F32),
            vmem((seq * rows, plan.group_out), BF16),
            vmem((fsdp, per_half, rows, plan.group_out), BF16),
            vmem((fsdp, rows, DIM), F32),
            vmem((fsdp, rows, DIM), BF16),
            vmem((rows, DIM), BF16),
            vmem((parts, *head_weight.shape[1:]), BF16),
            vmem((2 * PATCH, DIM), BF16),
            vmem((rows, DIM), F32),
            vmem((rows, 2 * PATCH), F32),
            vmem(latent.shape[2:], F32),
            vmem(latent.shape[2:], F32),
            dma((5,)),
            dma((chunks,)),
            dma((chunks, seq)),
            dma((chunks, seq)),
            dma,
            dma,
            dma((seq, fsdp)),
            dma((seq, fsdp)),
            dma,
            dma,
            dma((fsdp, seq)),
            dma((fsdp, seq)),
            dma((fsdp * (seq - 1),)),
            dma((fsdp * (seq - 1),)),
            dma((chunks, seq)),
            dma((chunks, fsdp, per_half)),
            dma((plan.blocks,)),
            dma((plan.blocks,)),
            dma,
            dma,
        ],
        compiler_params=pltpu.CompilerParams(
            collective_id=0, has_side_effects=True, vmem_limit_bytes=58 * 2**20
        ),
        name="fused_step",
    )(head_inputs, hidden, out_weight, time_weight, head_weight, latent, timesteps, freqs)
    return out[0].reshape(latent.shape), out[1].reshape(latent.shape)


def pick(mesh):
    seq, fsdp, sections = mesh.shape["seq"], mesh.shape["fsdp"], mesh.shape["section"]
    groups = mesh.shape["grp"]

    def run(*blocks):
        samples, rows = blocks[0].shape[1:3]
        fits = (
            samples == 1
            and fsdp == 2
            and sections == 2
            and groups == 2
            and seq & (seq - 1) == 0
            and seq % fsdp == 0
            and HEADS % seq == 0
            and (HEADS // seq * HEAD) % 128 == 0
            and rows % 16 == 0
            and seq * rows <= 512
            and DIM % 512 == 0
        )
        if fits:
            return fused_body(Plan(seq, fsdp, rows), *blocks)
        return body(*blocks)

    return run


def solution(mesh):
    return jax.shard_map(
        pick(mesh),
        mesh=mesh,
        in_specs=(
            P("section", ("grp", "fsdp"), "seq", None),
            P("section", ("grp", "fsdp"), "seq", None),
            P("section", "fsdp", None),
            P("section", None, ("seq", "fsdp")),
            P("section", ("seq", "fsdp"), None),
            P("section", ("grp", "fsdp"), "seq", None),
            P("section", ("grp", "fsdp"), None),
        ),
        out_specs=(
            P("section", ("grp", "fsdp"), "seq", None),
            P("section", ("grp", "fsdp"), "seq", None),
        ),
        check_vma=False,
    )
```
